32 devices in a mesh: tm: 16 (over z, y, x), chan: 2 (over core).
Axes of the slice: x: 2, y: 2, z: 4, core: 2. Of those that a mesh axis runs over, the one named last changes fastest.
Arguments:
- strain: bfloat16 [128, 131072], P('chan', 'tm'), as said below
- fir_taps: float32 [128, 64], P('chan'), may hold values from -0.75 to 0.75
Outputs:
- factor: float32 [1024, 1024], P(('tm', 'chan'))
- whitened: bfloat16 [1024, 16384], P(None, ('tm', 'chan'))
The draws below stay inside these ranges and needn't reach their ends.
Inputs may be any that keep to these rules, and one draw needn't show every extreme that they name: strain-rate samples of 128 channels.
All inputs are finite; a program needn't handle non-finite values.
Results may differ from the reference program's by a relative error of at most 0.001.
The reference program's roundings to bfloat16 on the way (of `decimated` and `hankel`) count: a program that leaves them out, or rounds other values in their place, can miss the bound.
Values may be sent and summed in bfloat16 or wider, within the bound.
A program may use at most 128 MiB of HBM per device.

```python
import math
import jax
import jax.numpy as jnp
from jax import lax

CH = 128
LAGS = 8
TAPS = 64
STRIDE = 8
TIME = 131072
ROWS_ALL = 16384


def draw_strain(key, part):
    key_noise, key_common, key_gain, key_rough = jax.random.split(key, 4)
    position = jnp.arange(TIME, dtype=jnp.float32)[None, :] / TIME
    rough = jnp.exp(jax.random.uniform(key_rough, (1, TIME), jnp.float32, -0.6, 0.6))
    noise = jnp.clip(jax.random.normal(key_noise, (CH, TIME), jnp.float32), -4.0, 4.0)
    common = jnp.clip(jax.random.normal(key_common, (1, TIME), jnp.float32), -4.0, 4.0)
    mixing = 0.5
    ramp = 1.0 + 2.0 * position
    gains = jnp.exp(jax.random.uniform(key_gain, (CH, 1), jnp.float32, 0.0, math.log(10.0)))
    values = gains * (ramp * rough) * (noise + mixing * common)
    return values.astype(jnp.bfloat16)


def steps_of(stream_key, dims, shards, low, top_value):
    level, own = 1.0, jax.random.fold_in(stream_key, 6)
    for dim, shards_of in shards:
        steps = jnp.exp(jax.random.uniform(jax.random.fold_in(own, dim), (shards_of,), jnp.float32, low / len(shards), top_value / len(shards)))
        level = level * jnp.repeat(steps, dims[dim] // shards_of).reshape([-1 if axis == dim else 1 for axis in range(len(dims))])
    return level


def scatter_about(own_key, extent, width, most, cuts=(), held_as=jnp.bfloat16):
    gain = steps_of(own_key, extent, cuts, -0.22, 0.18) if cuts else 1.0
    array = jax.random.normal(own_key, extent, jnp.float32) * width * gain
    return jnp.minimum(jnp.maximum(array, -most), most).astype(held_as)


def setup_inputs(seed: int = 0) -> dict:
    seeds = jax.random.split(jax.random.key(seed), 3)
    strain = draw_strain(jax.random.fold_in(seeds[2], 71), 0)
    fir_taps = scatter_about(seeds[1], (CH, TAPS), TAPS ** -0.5, 0.75, ((0, 2),), jnp.float32)
    return {"strain": strain, "fir_taps": fir_taps}


def decimate(extended, fir_taps, out_rows):
    channels = extended.shape[0]
    phases = jnp.transpose(extended.astype(jnp.float32).reshape(channels, -1, STRIDE), (0, 2, 1))
    running = jnp.zeros((channels, out_rows), jnp.float32)
    for j in range(TAPS // STRIDE):
        window = phases[:, :, j:j + out_rows]
        weights = fir_taps[:, j * STRIDE:(j + 1) * STRIDE].astype(jnp.float32)
        running = running + jnp.einsum('csn,cs->cn', window, weights, precision=lax.Precision.HIGHEST)
    return running

def reference(strain, fir_taps):
    extended = jnp.concatenate([strain, jnp.zeros((CH, TAPS - STRIDE), strain.dtype)], axis=1)
    decimated = decimate(extended, fir_taps, ROWS_ALL).astype(jnp.bfloat16)
    padded = jnp.concatenate([decimated, jnp.zeros((CH, LAGS - 1), jnp.bfloat16)], axis=1)
    hankel = jnp.concatenate([padded[:, i:i + ROWS_ALL] for i in range(LAGS)], axis=0)
    gram = lax.dot_general(hankel.astype(jnp.float32), hankel.astype(jnp.float32), (((1,), (1,)), ((), ())), preferred_element_type=jnp.float32)
    covariance = gram / ROWS_ALL
    lower_factor = jnp.linalg.cholesky(covariance)
    factor = lower_factor.T
    whitened = jax.scipy.linalg.solve_triangular(lower_factor, hankel.astype(jnp.float32), lower=True)
    return (factor, whitened.astype(jnp.bfloat16))
```

```python
import functools

import jax
import jax.numpy as jnp
from jax import lax
from jax.experimental import pallas as pl
from jax.experimental.pallas import tpu as pltpu
from jax.sharding import PartitionSpec as P

LAGS = 8
TAPS = 64
STRIDE = 8
LANES = 128
HIGHEST = lax.Precision.HIGHEST
VMEM = pl.BlockSpec(memory_space=pltpu.VMEM)


def shifted(value, axis, steps):
    count = lax.axis_size(axis)
    initial, last = (max(0, -steps), min(count, count - steps))
    return lax.ppermute(value, axis, [(source, source + steps) for source in range(initial, last)])


def decimate_kernel(strain_ref, rim_ref, taps_ref, out_ref, phase_ref):
    channels, samples = strain_ref.shape
    out_rows = samples // STRIDE
    width = STRIDE * LANES
    sample = lax.broadcasted_iota(jnp.int32, (width, width), 0)
    column = lax.broadcasted_iota(jnp.int32, (width, width), 1)
    wanted = STRIDE * (column % LANES) + column // LANES
    select = jnp.where(sample == wanted, 1.0, 0.0).astype(jnp.bfloat16)
    for g in range(out_rows // LANES + 1):
        if g < out_rows // LANES:
            part = jnp.dot(strain_ref[:, g * width : (g + 1) * width], select, preferred_element_type=jnp.float32)
        else:
            part = jnp.dot(rim_ref[...], select[:LANES], preferred_element_type=jnp.float32)
        for s in range(STRIDE):
            phase_ref[s, :, g * LANES : (g + 1) * LANES] = part[:, s * LANES : (s + 1) * LANES]
    span = out_rows + LANES
    for c in range(0, channels, 16):
        rows = slice(c, c + 16)
        total = jnp.zeros((16, span), jnp.float32)
        for j in range(TAPS // STRIDE):
            term = jnp.zeros((16, span), jnp.float32)
            for s in range(STRIDE):
                k = j * STRIDE + s
                term += taps_ref[rows, k : k + 1] * phase_ref[s, rows, :]
            total += term if j == 0 else pltpu.roll(term, span - j, 1)
        out_ref[rows, :] = total.astype(jnp.bfloat16)


def decimate(strain, rim, taps):
    channels, samples = strain.shape
    span = samples // STRIDE + LANES
    return pl.pallas_call(
        decimate_kernel,
        out_shape=jax.ShapeDtypeStruct((channels, span), jnp.bfloat16),
        in_specs=[VMEM] * 3,
        out_specs=VMEM,
        scratch_shapes=[pltpu.VMEM((STRIDE, channels, span), jnp.float32)],
        compiler_params=pltpu.CompilerParams(vmem_limit_bytes=40 * 2**20),
    )(strain, rim, taps)


def hankel_kernel(rows_ref, hankel_ref, sums_ref):
    group, first = lax.axis_index("tm"), lax.axis_index("chan")
    channels = rows_ref.shape[0]
    count = hankel_ref.shape[1]
    start = pl.multiple_of(first * count, LANES)
    window = rows_ref[:, pl.ds(start, count + LANES)].astype(jnp.float32)
    span = count + LANES
    for i in range(LAGS):
        moved = window if i == 0 else pltpu.roll(window, span - i, 1)
        hankel_ref[i * channels : (i + 1) * channels, :] = moved[:, :count].astype(jnp.bfloat16)
    leads = jnp.logical_and(group == 0, first == 0)
    skip = jnp.where(leads, LAGS - 1, 0)
    keep = lax.broadcasted_iota(jnp.int32, (channels, count), 1) >= skip
    left = jnp.where(keep, window[:, :count], 0.0).astype(jnp.bfloat16)
    sums_ref[:, : LAGS * channels] = lax.dot_general(
        left, hankel_ref[...], (((1,), (1,)), ((), ())), preferred_element_type=jnp.float32
    )
    lane = lax.broadcasted_iota(jnp.int32, (channels, LANES), 1)
    seen = jnp.where(leads, 2 * LAGS, 0)
    sums_ref[:, LAGS * channels :] = jnp.where(lane < seen, window[:, :LANES], 0.0)


def hankel_and_sums(rows, count):
    channels = rows.shape[0]
    return pl.pallas_call(
        hankel_kernel,
        out_shape=(
            jax.ShapeDtypeStruct((LAGS * channels, count), jnp.bfloat16),
            jax.ShapeDtypeStruct((channels, LAGS * channels + LANES), jnp.float32),
        ),
        in_specs=[VMEM],
        out_specs=(VMEM, VMEM),
        compiler_params=pltpu.CompilerParams(vmem_limit_bytes=40 * 2**20),
    )(rows)


def factor_block(block):
    size = block.shape[0]
    row_id = lax.broadcasted_iota(jnp.int32, (size, size), 0)
    col_id = lax.broadcasted_iota(jnp.int32, (size, size), 1)
    sub = lax.broadcasted_iota(jnp.int32, (8, size), 0)
    low = block
    inv = jnp.where(row_id == col_id, 1.0, 0.0)
    factors, inverses = [], []
    for b in range(size // 8):
        cols = [jnp.broadcast_to(low[:, 8 * b + j : 8 * b + j + 1], low.shape) for j in range(8)]
        top, low = low[:8], low[8:]
        x_top, inv = inv[:8], inv[8:]
        c_top, c_low = [c[:8] for c in cols], [c[8:] for c in cols]
        scale = jnp.zeros((8, size), jnp.float32)
        more = b < size // 8 - 1
        for i in range(8):
            root = lax.rsqrt(jnp.broadcast_to(c_top[i][i : i + 1], (8, size)))
            over = root[:1] * root[:1]
            scale = jnp.where(sub == i, root, scale)
            below = jnp.where(sub > i, c_top[i], 0.0)
            row, x_row = top[i : i + 1] * over, x_top[i : i + 1] * over
            c_row = [c_top[j][i : i + 1] * over for j in range(i + 1, 8)]
            top, x_top = top - below * row, x_top - below * x_row
            for j in range(i + 1, 8):
                c_top[j] = c_top[j] - below * c_row[j - i - 1]
            if more:
                low, inv = low - c_low[i] * row, inv - c_low[i] * x_row
                for j in range(i + 1, 8):
                    c_low[j] = c_low[j] - c_low[i] * c_row[j - i - 1]
        factors.append(top * scale)
        inverses.append(x_top * scale)
    factor = jnp.concatenate(factors, axis=0)
    return jnp.where(col_id >= row_id, factor, 0.0), jnp.concatenate(inverses, axis=0)


def whiten_kernel(rows_all, sums_ref, hankel_ref, factor_ref, white_ref, work_ref):
    columns, count = hankel_ref.shape
    channels = columns // LAGS
    size = channels
    head = sums_ref[:, columns:]
    lane = lax.broadcasted_iota(jnp.int32, (channels, LANES), 1)
    heads = [(head if i == 0 else pltpu.roll(head, LANES - i, 1)).astype(jnp.bfloat16) for i in range(LAGS)]
    head_hankel = jnp.concatenate(heads, axis=0)
    scale = 1.0 / rows_all
    for i in range(LAGS):
        wide = columns - i * channels
        own = jnp.logical_and(lane >= i, lane < LAGS - 1)
        left = jnp.where(own, head, 0.0).astype(jnp.bfloat16)
        extra = lax.dot_general(
            left, head_hankel[:wide], (((1,), (1,)), ((), ())), preferred_element_type=jnp.float32
        )
        work_ref[i * channels : (i + 1) * channels, i * channels : columns] = (sums_ref[:, :wide] + extra) * scale
        if i:
            work_ref[i * channels : (i + 1) * channels, : i * channels] = jnp.zeros((channels, i * channels), jnp.float32)
    work_ref[:, columns:] = hankel_ref[...].astype(jnp.float32)

    def step(k, _):
        first = pl.multiple_of(k * size, size)
        mine = pl.ds(first, size)
        factor, inverse = factor_block(work_ref[mine, mine])
        solved = jnp.dot(inverse, work_ref[mine, :], preferred_element_type=jnp.float32, precision=HIGHEST)
        work_ref[mine, :] = solved
        work_ref[mine, mine] = factor
        white_ref[mine, :] = solved[:, columns:].astype(jnp.bfloat16)

        def update(i, _):
            other = pl.ds(pl.multiple_of(i * size, size), size)
            work_ref[other, :] -= lax.dot_general(
                work_ref[mine, other],
                work_ref[mine, :],
                (((0,), (0,)), ((), ())),
                preferred_element_type=jnp.float32,
                precision=HIGHEST,
            )
            return 0

        lax.fori_loop(k + 1, LAGS, update, 0)
        return 0

    lax.fori_loop(0, LAGS, step, 0)
    kept = factor_ref.shape[0]
    me = lax.axis_index("tm") * lax.axis_size("chan") + lax.axis_index("chan")
    first_row = pl.multiple_of(me * (columns // (lax.axis_size("tm") * lax.axis_size("chan"))) // kept * kept, kept)
    rows = work_ref[pl.ds(first_row, kept), :columns]
    row_id = lax.broadcasted_iota(jnp.int32, rows.shape, 0) + first_row
    col_id = lax.broadcasted_iota(jnp.int32, rows.shape, 1)
    factor_ref[...] = jnp.where(col_id >= row_id, rows, 0.0)


def whiten(sums, hankel, rows_all, kept):
    columns, count = hankel.shape
    return pl.pallas_call(
        functools.partial(whiten_kernel, rows_all),
        out_shape=(
            jax.ShapeDtypeStruct((kept, columns), jnp.float32),
            jax.ShapeDtypeStruct((columns, count), jnp.bfloat16),
        ),
        in_specs=[VMEM, VMEM],
        out_specs=(VMEM, VMEM),
        scratch_shapes=[pltpu.VMEM((columns, columns + count), jnp.float32)],
        compiler_params=pltpu.CompilerParams(vmem_limit_bytes=48 * 2**20),
    )(sums, hankel)


def local(strain, fir_taps):
    samples = strain.shape[1]
    out_rows = samples // STRIDE
    rim = shifted(strain[:, :LANES], "tm", -1)
    decimated = decimate(strain, rim, fir_taps)
    gathered = lax.all_gather(decimated, "chan", axis=0, tiled=True)
    row_count = out_rows // lax.axis_size("chan")
    hankel, sums = hankel_and_sums(gathered, row_count)
    sums = lax.psum(sums, ("tm", "chan"))
    devices_all = lax.axis_size(("tm", "chan"))
    columns = hankel.shape[0]
    factor_rows = columns // devices_all
    kept = max(8, factor_rows)
    factor, whitened = whiten(sums, hankel, row_count * devices_all, kept)
    if kept > factor_rows:
        first_row = lax.axis_index(("tm", "chan")) * factor_rows % kept
        factor = lax.dynamic_slice_in_dim(factor, first_row, factor_rows, 0)
    return (factor, whitened)


def solution(mesh):
    placed = (P("chan", "tm"), P("chan", None))
    return jax.shard_map(
        local,
        mesh=mesh,
        in_specs=placed,
        out_specs=(P(("tm", "chan"), None), P(None, ("tm", "chan"))),
        check_vma=False,
    )
```

```python
import functools

import jax
import jax.numpy as jnp
from jax import lax
from jax.experimental import pallas as pl
from jax.experimental.pallas import tpu as pltpu
from jax.sharding import PartitionSpec as P

LAGS = 8
TAPS = 64
STRIDE = 8
LANES = 128
MESH = pl.DeviceIdType.MESH
HIGHEST = lax.Precision.HIGHEST
VMEM = pl.BlockSpec(memory_space=pltpu.VMEM)


def shifted(value, axis, steps):
    count = lax.axis_size(axis)
    initial, last = (max(0, -steps), min(count, count - steps))
    return lax.ppermute(value, axis, [(source, source + steps) for source in range(initial, last)])


def decimate_kernel(strain_ref, rim_ref, taps_ref, out_ref, phase_ref):
    channels, samples = strain_ref.shape
    out_rows = samples // STRIDE
    width = STRIDE * LANES
    sample = lax.broadcasted_iota(jnp.int32, (width, width), 0)
    column = lax.broadcasted_iota(jnp.int32, (width, width), 1)
    wanted = STRIDE * (column % LANES) + column // LANES
    select = jnp.where(sample == wanted, 1.0, 0.0).astype(jnp.bfloat16)
    for g in range(out_rows // LANES + 1):
        if g < out_rows // LANES:
            part = jnp.dot(strain_ref[:, g * width : (g + 1) * width], select, preferred_element_type=jnp.float32)
        else:
            part = jnp.dot(rim_ref[...], select[:LANES], preferred_element_type=jnp.float32)
        for s in range(STRIDE):
            phase_ref[s, :, g * LANES : (g + 1) * LANES] = part[:, s * LANES : (s + 1) * LANES]
    span = out_rows + LANES
    for c in range(0, channels, 16):
        rows = slice(c, c + 16)
        total = jnp.zeros((16, span), jnp.float32)
        for j in range(TAPS // STRIDE):
            term = jnp.zeros((16, span), jnp.float32)
            for s in range(STRIDE):
                k = j * STRIDE + s
                term += taps_ref[rows, k : k + 1] * phase_ref[s, rows, :]
            total += term if j == 0 else pltpu.roll(term, span - j, 1)
        out_ref[rows, :] = total.astype(jnp.bfloat16)


def decimate(strain, rim, taps):
    channels, samples = strain.shape
    span = samples // STRIDE + LANES
    return pl.pallas_call(
        decimate_kernel,
        out_shape=jax.ShapeDtypeStruct((channels, span), jnp.bfloat16),
        in_specs=[VMEM] * 3,
        out_specs=VMEM,
        scratch_shapes=[pltpu.VMEM((STRIDE, channels, span), jnp.float32)],
        compiler_params=pltpu.CompilerParams(vmem_limit_bytes=40 * 2**20),
    )(strain, rim, taps)


def hankel_kernel(rows_ref, hankel_ref, sums_ref):
    group, first = lax.axis_index("tm"), lax.axis_index("chan")
    channels = rows_ref.shape[0]
    count = hankel_ref.shape[1]
    start = pl.multiple_of(first * count, LANES)
    window = rows_ref[:, pl.ds(start, count + LANES)].astype(jnp.float32)
    span = count + LANES
    for i in range(LAGS):
        moved = window if i == 0 else pltpu.roll(window, span - i, 1)
        hankel_ref[i * channels : (i + 1) * channels, :] = moved[:, :count].astype(jnp.bfloat16)
    leads = jnp.logical_and(group == 0, first == 0)
    skip = jnp.where(leads, LAGS - 1, 0)
    keep = lax.broadcasted_iota(jnp.int32, (channels, count), 1) >= skip
    left = jnp.where(keep, window[:, :count], 0.0).astype(jnp.bfloat16)
    sums_ref[:, : LAGS * channels] = lax.dot_general(
        left, hankel_ref[...], (((1,), (1,)), ((), ())), preferred_element_type=jnp.float32
    )
    lane = lax.broadcasted_iota(jnp.int32, (channels, LANES), 1)
    seen = jnp.where(leads, 2 * LAGS, 0)
    sums_ref[:, LAGS * channels :] = jnp.where(lane < seen, window[:, :LANES], 0.0)


def hankel_and_sums(rows, count):
    channels = rows.shape[0]
    return pl.pallas_call(
        hankel_kernel,
        out_shape=(
            jax.ShapeDtypeStruct((LAGS * channels, count), jnp.bfloat16),
            jax.ShapeDtypeStruct((channels, LAGS * channels + LANES), jnp.float32),
        ),
        in_specs=[VMEM],
        out_specs=(VMEM, VMEM),
        compiler_params=pltpu.CompilerParams(vmem_limit_bytes=40 * 2**20),
    )(rows)


def sum_kernel(near, mine_ref, out_ref, total, from_core, from_near, from_far, full, core_sem, near_sem, far_sem, all_sem, hand_sem):
    tm, chan = lax.axis_index("tm"), lax.axis_index("chan")
    far = lax.axis_size("tm") // near
    spot, place = lax.rem(tm, near), lax.div(tm, near)
    rows = mine_ref.shape[0]
    half = rows // 2
    piece = half // near
    core = {"chan": 1 - chan}

    def near_of(d):
        return lax.rem(spot + d, near)

    def near_id(d):
        return {"tm": place * near + near_of(d)}

    def far_id(d):
        return {"tm": lax.rem(place + d, far) * near + spot}

    def copy(source, target, sems, slot, device):
        return pltpu.make_async_remote_copy(
            src_ref=source,
            dst_ref=target,
            send_sem=sems.at[0, slot],
            recv_sem=sems.at[1, slot],
            device_id=device,
            device_id_type=MESH,
        )

    barrier = pltpu.get_barrier_semaphore()
    partners = [core] + [near_id(d) for d in range(1, near)] + [far_id(d) for d in range(1, far)]
    for partner in partners:
        pl.semaphore_signal(barrier, inc=1, device_id=partner, device_id_type=MESH)
    pl.semaphore_wait(barrier, len(partners))

    away = pl.ds(pl.multiple_of((1 - chan) * half, half), half)
    home = pl.ds(pl.multiple_of(chan * half, half), half)
    step = copy(mine_ref.at[away], from_core, core_sem, 0, core)
    step.start()
    step.wait()
    total[...] = mine_ref[home] + from_core[...]

    steps = []
    for d in range(1, near):
        part = total.at[pl.ds(pl.multiple_of(near_of(d) * piece, piece), piece)]
        steps.append(copy(part, from_near.at[d - 1], near_sem, d - 1, near_id(d)))
        steps[-1].start()
    own = total[pl.ds(pl.multiple_of(spot * piece, piece), piece)]
    for d in range(1, near):
        steps[d - 1].wait()
        own += from_near[d - 1]

    from_far[place] = own
    steps = []
    for d in range(1, far):
        steps.append(copy(from_far.at[place], from_far.at[place], far_sem, d - 1, far_id(d)))
        steps[-1].start()
    for step in steps:
        step.wait()
    own = from_far[0]
    for d in range(1, far):
        own += from_far[d]

    def at(spot_of):
        return pl.ds(pl.multiple_of(chan * half + spot_of * piece, piece), piece)

    full[at(spot)] = own
    steps = []
    for d in range(1, near):
        steps.append(copy(full.at[at(spot)], full.at[at(spot)], all_sem, d - 1, near_id(d)))
        steps[-1].start()
    hands = [copy(full.at[at(spot)], full.at[at(spot)], hand_sem, 0, core)]
    hands[0].start()
    for d in range(1, near):
        steps[d - 1].wait()
        came = at(lax.rem(spot - d + near, near))
        hands.append(copy(full.at[came], full.at[came], hand_sem, d, core))
        hands[-1].start()
    for hand in hands:
        hand.wait()
    out_ref[...] = full[...]


def summed(value):
    rows, columns = value.shape
    tm = lax.axis_size("tm")
    near = 4 if tm % 4 == 0 else 2
    far = tm // near
    half, piece = rows // 2, rows // 2 // near
    dtype = jnp.float32
    return pl.pallas_call(
        functools.partial(sum_kernel, near),
        out_shape=jax.ShapeDtypeStruct((rows, columns), dtype),
        in_specs=[VMEM],
        out_specs=VMEM,
        scratch_shapes=[
            pltpu.VMEM((half, columns), dtype),
            pltpu.VMEM((half, columns), dtype),
            pltpu.VMEM((near - 1, piece, columns), dtype),
            pltpu.VMEM((far, piece, columns), dtype),
            pltpu.VMEM((rows, columns), dtype),
            pltpu.SemaphoreType.DMA((2, 1)),
            pltpu.SemaphoreType.DMA((2, near - 1)),
            pltpu.SemaphoreType.DMA((2, max(far - 1, 1))),
            pltpu.SemaphoreType.DMA((2, near - 1)),
            pltpu.SemaphoreType.DMA((2, near)),
        ],
        compiler_params=pltpu.CompilerParams(
            collective_id=0, has_side_effects=True, vmem_limit_bytes=24 * 2**20
        ),
    )(value)


def factor_block(block):
    size = block.shape[0]
    row_id = lax.broadcasted_iota(jnp.int32, (size, size), 0)
    col_id = lax.broadcasted_iota(jnp.int32, (size, size), 1)
    sub = lax.broadcasted_iota(jnp.int32, (8, size), 0)
    low = block
    inv = jnp.where(row_id == col_id, 1.0, 0.0)
    factors, inverses = [], []
    for b in range(size // 8):
        cols = [jnp.broadcast_to(low[:, 8 * b + j : 8 * b + j + 1], low.shape) for j in range(8)]
        top, low = low[:8], low[8:]
        x_top, inv = inv[:8], inv[8:]
        c_top, c_low = [c[:8] for c in cols], [c[8:] for c in cols]
        scale = jnp.zeros((8, size), jnp.float32)
        more = b < size // 8 - 1
        for i in range(8):
            root = lax.rsqrt(jnp.broadcast_to(c_top[i][i : i + 1], (8, size)))
            over = root[:1] * root[:1]
            scale = jnp.where(sub == i, root, scale)
            below = jnp.where(sub > i, c_top[i], 0.0)
            row, x_row = top[i : i + 1] * over, x_top[i : i + 1] * over
            c_row = [c_top[j][i : i + 1] * over for j in range(i + 1, 8)]
            top, x_top = top - below * row, x_top - below * x_row
            for j in range(i + 1, 8):
                c_top[j] = c_top[j] - below * c_row[j - i - 1]
            if more:
                low, inv = low - c_low[i] * row, inv - c_low[i] * x_row
                for j in range(i + 1, 8):
                    c_low[j] = c_low[j] - c_low[i] * c_row[j - i - 1]
        factors.append(top * scale)
        inverses.append(x_top * scale)
    factor = jnp.concatenate(factors, axis=0)
    return jnp.where(col_id >= row_id, factor, 0.0), jnp.concatenate(inverses, axis=0)


def whiten_kernel(rows_all, sums_ref, hankel_ref, factor_ref, white_ref, work_ref):
    columns, count = hankel_ref.shape
    channels = columns // LAGS
    size = channels
    head = sums_ref[:, columns:]
    lane = lax.broadcasted_iota(jnp.int32, (channels, LANES), 1)
    heads = [(head if i == 0 else pltpu.roll(head, LANES - i, 1)).astype(jnp.bfloat16) for i in range(LAGS)]
    head_hankel = jnp.concatenate(heads, axis=0)
    scale = 1.0 / rows_all
    for i in range(LAGS):
        wide = columns - i * channels
        own = jnp.logical_and(lane >= i, lane < LAGS - 1)
        left = jnp.where(own, head, 0.0).astype(jnp.bfloat16)
        extra = lax.dot_general(
            left, head_hankel[:wide], (((1,), (1,)), ((), ())), preferred_element_type=jnp.float32
        )
        work_ref[i * channels : (i + 1) * channels, i * channels : columns] = (sums_ref[:, :wide] + extra) * scale
        if i:
            work_ref[i * channels : (i + 1) * channels, : i * channels] = jnp.zeros((channels, i * channels), jnp.float32)
    work_ref[:, columns:] = hankel_ref[...].astype(jnp.float32)

    def step(k, _):
        first = pl.multiple_of(k * size, size)
        mine = pl.ds(first, size)
        factor, inverse = factor_block(work_ref[mine, mine])
        solved = jnp.dot(inverse, work_ref[mine, :], preferred_element_type=jnp.float32, precision=HIGHEST)
        work_ref[mine, :] = solved
        work_ref[mine, mine] = factor
        white_ref[mine, :] = solved[:, columns:].astype(jnp.bfloat16)

        def update(i, _):
            other = pl.ds(pl.multiple_of(i * size, size), size)
            work_ref[other, :] -= lax.dot_general(
                work_ref[mine, other],
                work_ref[mine, :],
                (((0,), (0,)), ((), ())),
                preferred_element_type=jnp.float32,
                precision=HIGHEST,
            )
            return 0

        lax.fori_loop(k + 1, LAGS, update, 0)
        return 0

    lax.fori_loop(0, LAGS, step, 0)
    kept = factor_ref.shape[0]
    me = lax.axis_index("tm") * lax.axis_size("chan") + lax.axis_index("chan")
    first_row = pl.multiple_of(me * (columns // (lax.axis_size("tm") * lax.axis_size("chan"))) // kept * kept, kept)
    rows = work_ref[pl.ds(first_row, kept), :columns]
    row_id = lax.broadcasted_iota(jnp.int32, rows.shape, 0) + first_row
    col_id = lax.broadcasted_iota(jnp.int32, rows.shape, 1)
    factor_ref[...] = jnp.where(col_id >= row_id, rows, 0.0)


def whiten(sums, hankel, rows_all, kept):
    columns, count = hankel.shape
    return pl.pallas_call(
        functools.partial(whiten_kernel, rows_all),
        out_shape=(
            jax.ShapeDtypeStruct((kept, columns), jnp.float32),
            jax.ShapeDtypeStruct((columns, count), jnp.bfloat16),
        ),
        in_specs=[VMEM, VMEM],
        out_specs=(VMEM, VMEM),
        scratch_shapes=[pltpu.VMEM((columns, columns + count), jnp.float32)],
        compiler_params=pltpu.CompilerParams(vmem_limit_bytes=48 * 2**20),
    )(sums, hankel)


def local(strain, fir_taps):
    samples = strain.shape[1]
    out_rows = samples // STRIDE
    rim = shifted(strain[:, :LANES], "tm", -1)
    decimated = decimate(strain, rim, fir_taps)
    gathered = lax.all_gather(decimated, "chan", axis=0, tiled=True)
    row_count = out_rows // lax.axis_size("chan")
    hankel, sums = hankel_and_sums(gathered, row_count)
    sums = summed(sums)
    devices_all = lax.axis_size(("tm", "chan"))
    columns = hankel.shape[0]
    factor_rows = columns // devices_all
    kept = max(8, factor_rows)
    factor, whitened = whiten(sums, hankel, row_count * devices_all, kept)
    if kept > factor_rows:
        first_row = lax.axis_index(("tm", "chan")) * factor_rows % kept
        factor = lax.dynamic_slice_in_dim(factor, first_row, factor_rows, 0)
    return (factor, whitened)


def solution(mesh):
    placed = (P("chan", "tm"), P("chan", None))
    return jax.shard_map(
        local,
        mesh=mesh,
        in_specs=placed,
        out_specs=(P(("tm", "chan"), None), P(None, ("tm", "chan"))),
        check_vma=False,
    )
```

```python
import functools

import jax
import jax.numpy as jnp
from jax import lax
from jax.experimental import pallas as pl
from jax.experimental.pallas import tpu as pltpu
from jax.sharding import PartitionSpec as P

LAGS = 8
TAPS = 64
STRIDE = 8
LANES = 128
MESH = pl.DeviceIdType.MESH
HIGHEST = lax.Precision.HIGHEST
VMEM = pl.BlockSpec(memory_space=pltpu.VMEM)


def shifted(value, axis, steps):
    count = lax.axis_size(axis)
    initial, last = (max(0, -steps), min(count, count - steps))
    return lax.ppermute(value, axis, [(source, source + steps) for source in range(initial, last)])


def decimate_kernel(strain_ref, rim_ref, taps_ref, out_ref, phase_ref):
    channels, samples = strain_ref.shape
    out_rows = samples // STRIDE
    width = STRIDE * LANES
    sample = lax.broadcasted_iota(jnp.int32, (width, width), 0)
    column = lax.broadcasted_iota(jnp.int32, (width, width), 1)
    wanted = STRIDE * (column % LANES) + column // LANES
    select = jnp.where(sample == wanted, 1.0, 0.0).astype(jnp.bfloat16)
    for g in range(out_rows // LANES + 1):
        if g < out_rows // LANES:
            part = jnp.dot(strain_ref[:, g * width : (g + 1) * width], select, preferred_element_type=jnp.float32)
        else:
            part = jnp.dot(rim_ref[...], select[:LANES], preferred_element_type=jnp.float32)
        for s in range(STRIDE):
            phase_ref[s, :, g * LANES : (g + 1) * LANES] = part[:, s * LANES : (s + 1) * LANES]
    span = out_rows + LANES
    for c in range(0, channels, 16):
        rows = slice(c, c + 16)
        total = jnp.zeros((16, span), jnp.float32)
        for j in range(TAPS // STRIDE):
            term = jnp.zeros((16, span), jnp.float32)
            for s in range(STRIDE):
                k = j * STRIDE + s
                term += taps_ref[rows, k : k + 1] * phase_ref[s, rows, :]
            total += term if j == 0 else pltpu.roll(term, span - j, 1)
        out_ref[rows, :] = total.astype(jnp.bfloat16)


def decimate(strain, rim, taps):
    channels, samples = strain.shape
    span = samples // STRIDE + LANES
    return pl.pallas_call(
        decimate_kernel,
        out_shape=jax.ShapeDtypeStruct((channels, span), jnp.bfloat16),
        in_specs=[VMEM] * 3,
        out_specs=VMEM,
        scratch_shapes=[pltpu.VMEM((STRIDE, channels, span), jnp.float32)],
        compiler_params=pltpu.CompilerParams(vmem_limit_bytes=40 * 2**20),
    )(strain, rim, taps)


def hankel_kernel(rows_ref, hankel_ref, sums_ref):
    group, first = lax.axis_index("tm"), lax.axis_index("chan")
    channels = rows_ref.shape[0]
    count = hankel_ref.shape[1]
    start = pl.multiple_of(first * count, LANES)
    window = rows_ref[:, pl.ds(start, count + LANES)].astype(jnp.float32)
    span = count + LANES
    for i in range(LAGS):
        moved = window if i == 0 else pltpu.roll(window, span - i, 1)
        hankel_ref[i * channels : (i + 1) * channels, :] = moved[:, :count].astype(jnp.bfloat16)
    leads = jnp.logical_and(group == 0, first == 0)
    skip = jnp.where(leads, LAGS - 1, 0)
    keep = lax.broadcasted_iota(jnp.int32, (channels, count), 1) >= skip
    left = jnp.where(keep, window[:, :count], 0.0).astype(jnp.bfloat16)
    sums_ref[:, : LAGS * channels] = lax.dot_general(
        left, hankel_ref[...], (((1,), (1,)), ((), ())), preferred_element_type=jnp.float32
    )
    lane = lax.broadcasted_iota(jnp.int32, (channels, LANES), 1)
    seen = jnp.where(leads, 2 * LAGS, 0)
    sums_ref[:, LAGS * channels :] = jnp.where(lane < seen, window[:, :LANES], 0.0)


def hankel_and_sums(rows, count):
    channels = rows.shape[0]
    return pl.pallas_call(
        hankel_kernel,
        out_shape=(
            jax.ShapeDtypeStruct((LAGS * channels, count), jnp.bfloat16),
            jax.ShapeDtypeStruct((channels, LAGS * channels + LANES), jnp.float32),
        ),
        in_specs=[VMEM],
        out_specs=(VMEM, VMEM),
        compiler_params=pltpu.CompilerParams(vmem_limit_bytes=40 * 2**20),
    )(rows)


def sum_kernel(near, mine_ref, out_ref, total, from_core, from_near, from_far, full, core_sem, near_sem, far_sem, all_sem, hand_sem):
    tm, chan = lax.axis_index("tm"), lax.axis_index("chan")
    far = lax.axis_size("tm") // near
    spot, place = lax.rem(tm, near), lax.div(tm, near)
    rows = mine_ref.shape[0]
    half = rows // 2
    piece = half // near
    core = {"chan": 1 - chan}

    def near_of(d):
        return lax.rem(spot + d, near)

    def near_id(d):
        return {"tm": place * near + near_of(d)}

    def far_id(d):
        return {"tm": lax.rem(place + d, far) * near + spot}

    def copy(source, target, sems, slot, device):
        return pltpu.make_async_remote_copy(
            src_ref=source,
            dst_ref=target,
            send_sem=sems.at[0, slot],
            recv_sem=sems.at[1, slot],
            device_id=device,
            device_id_type=MESH,
        )

    barrier = pltpu.get_barrier_semaphore()
    partners = [core] + [near_id(d) for d in range(1, near)] + [far_id(d) for d in range(1, far)]
    for partner in partners:
        pl.semaphore_signal(barrier, inc=1, device_id=partner, device_id_type=MESH)
    pl.semaphore_wait(barrier, len(partners))

    away = pl.ds(pl.multiple_of((1 - chan) * half, half), half)
    home = pl.ds(pl.multiple_of(chan * half, half), half)
    step = copy(mine_ref.at[away], from_core, core_sem, 0, core)
    step.start()
    step.wait()
    total[...] = mine_ref[home] + from_core[...]

    steps = []
    for d in range(1, near):
        part = total.at[pl.ds(pl.multiple_of(near_of(d) * piece, piece), piece)]
        steps.append(copy(part, from_near.at[d - 1], near_sem, d - 1, near_id(d)))
        steps[-1].start()
    own = total[pl.ds(pl.multiple_of(spot * piece, piece), piece)]
    for d in range(1, near):
        steps[d - 1].wait()
        own += from_near[d - 1]

    from_far[place] = own
    steps = []
    for d in range(1, far):
        steps.append(copy(from_far.at[place], from_far.at[place], far_sem, d - 1, far_id(d)))
        steps[-1].start()
    for step in steps:
        step.wait()
    own = from_far[0]
    for d in range(1, far):
        own += from_far[d]

    def at(spot_of):
        return pl.ds(pl.multiple_of(chan * half + spot_of * piece, piece), piece)

    full[at(spot)] = own
    steps = []
    for d in range(1, near):
        steps.append(copy(full.at[at(spot)], full.at[at(spot)], all_sem, d - 1, near_id(d)))
        steps[-1].start()
    hands = [copy(full.at[at(spot)], full.at[at(spot)], hand_sem, 0, core)]
    hands[0].start()
    for d in range(1, near):
        steps[d - 1].wait()
        came = at(lax.rem(spot - d + near, near))
        hands.append(copy(full.at[came], full.at[came], hand_sem, d, core))
        hands[-1].start()
    for hand in hands:
        hand.wait()
    out_ref[...] = full[...]


def summed(value):
    rows, columns = value.shape
    tm = lax.axis_size("tm")
    near = 4 if tm % 4 == 0 else 2
    far = tm // near
    half, piece = rows // 2, rows // 2 // near
    dtype = jnp.float32
    return pl.pallas_call(
        functools.partial(sum_kernel, near),
        out_shape=jax.ShapeDtypeStruct((rows, columns), dtype),
        in_specs=[VMEM],
        out_specs=VMEM,
        scratch_shapes=[
            pltpu.VMEM((half, columns), dtype),
            pltpu.VMEM((half, columns), dtype),
            pltpu.VMEM((near - 1, piece, columns), dtype),
            pltpu.VMEM((far, piece, columns), dtype),
            pltpu.VMEM((rows, columns), dtype),
            pltpu.SemaphoreType.DMA((2, 1)),
            pltpu.SemaphoreType.DMA((2, near - 1)),
            pltpu.SemaphoreType.DMA((2, max(far - 1, 1))),
            pltpu.SemaphoreType.DMA((2, near - 1)),
            pltpu.SemaphoreType.DMA((2, near)),
        ],
        compiler_params=pltpu.CompilerParams(
            collective_id=0, has_side_effects=True, vmem_limit_bytes=24 * 2**20
        ),
    )(value)


def factor_block(block):
    size = block.shape[0]
    row_id = lax.broadcasted_iota(jnp.int32, (size, size), 0)
    col_id = lax.broadcasted_iota(jnp.int32, (size, size), 1)
    sub = lax.broadcasted_iota(jnp.int32, (8, size), 0)
    low = block
    inv = jnp.where(row_id == col_id, 1.0, 0.0)
    factors, inverses = [], []
    for b in range(size // 8):
        cols = [jnp.broadcast_to(low[:, 8 * b + j : 8 * b + j + 1], low.shape) for j in range(8)]
        top, low = low[:8], low[8:]
        x_top, inv = inv[:8], inv[8:]
        c_top, c_low = [c[:8] for c in cols], [c[8:] for c in cols]
        scale = jnp.zeros((8, size), jnp.float32)
        more = b < size // 8 - 1
        for i in range(8):
            root = lax.rsqrt(jnp.broadcast_to(c_top[i][i : i + 1], (8, size)))
            over = root[:1] * root[:1]
            scale = jnp.where(sub == i, root, scale)
            below = jnp.where(sub > i, c_top[i], 0.0)
            row, x_row = top[i : i + 1] * over, x_top[i : i + 1] * over
            c_row = [c_top[j][i : i + 1] * over for j in range(i + 1, 8)]
            top, x_top = top - below * row, x_top - below * x_row
            for j in range(i + 1, 8):
                c_top[j] = c_top[j] - below * c_row[j - i - 1]
            if more:
                low, inv = low - c_low[i] * row, inv - c_low[i] * x_row
                for j in range(i + 1, 8):
                    c_low[j] = c_low[j] - c_low[i] * c_row[j - i - 1]
        factors.append(top * scale)
        inverses.append(x_top * scale)
    factor = jnp.concatenate(factors, axis=0)
    return jnp.where(col_id >= row_id, factor, 0.0), jnp.concatenate(inverses, axis=0)


def whiten_kernel(rows_all, sums_ref, hankel_ref, factor_ref, white_ref, work_ref, left_ref, right_ref):
    columns, count = hankel_ref.shape
    channels = columns // LAGS
    size = channels
    head = sums_ref[:, columns:]
    lane = lax.broadcasted_iota(jnp.int32, (channels, LANES), 1)
    heads = [(head if i == 0 else pltpu.roll(head, LANES - i, 1)).astype(jnp.bfloat16) for i in range(LAGS)]
    head_hankel = jnp.concatenate(heads, axis=0)
    scale = 1.0 / rows_all
    for i in range(LAGS):
        wide = columns - i * channels
        own = jnp.logical_and(lane >= i, lane < LAGS - 1)
        left = jnp.where(own, head, 0.0).astype(jnp.bfloat16)
        extra = lax.dot_general(
            left, head_hankel[:wide], (((1,), (1,)), ((), ())), preferred_element_type=jnp.float32
        )
        work_ref[i * channels : (i + 1) * channels, i * channels : columns] = (sums_ref[:, :wide] + extra) * scale
        if i:
            work_ref[i * channels : (i + 1) * channels, : i * channels] = jnp.zeros((channels, i * channels), jnp.float32)
    work_ref[:, columns:] = hankel_ref[...].astype(jnp.float32)

    def step(k, _):
        first = pl.multiple_of(k * size, size)
        mine = pl.ds(first, size)
        factor, inverse = factor_block(work_ref[mine, mine])
        solved = jnp.dot(inverse, work_ref[mine, :], preferred_element_type=jnp.float32, precision=HIGHEST)
        work_ref[mine, :] = solved
        work_ref[mine, mine] = factor
        white_ref[mine, :] = solved[:, columns:].astype(jnp.bfloat16)

        high = solved.astype(jnp.bfloat16)
        rest = solved - high.astype(jnp.float32)
        middle = rest.astype(jnp.bfloat16)
        little = (rest - middle.astype(jnp.float32)).astype(jnp.bfloat16)
        for n, (left, right) in enumerate(
            ((high, high), (high, middle), (middle, high), (middle, middle), (high, little), (little, high))
        ):
            left_ref[n * size : (n + 1) * size, :] = left[:, :columns]
            right_ref[n * size : (n + 1) * size, :] = right

        def update(start, i, _):
            other = pl.ds(pl.multiple_of(i * size, size), size)
            work_ref[other, start:] -= lax.dot_general(
                left_ref[:, other],
                right_ref[:, start:],
                (((0,), (0,)), ((), ())),
                preferred_element_type=jnp.float32,
            )
            return 0

        middle_lag = LAGS // 2
        lax.fori_loop(k + 1, middle_lag, functools.partial(update, 0), 0)
        lax.fori_loop(
            jnp.maximum(k + 1, middle_lag), LAGS, functools.partial(update, middle_lag * size), 0
        )
        return 0

    lax.fori_loop(0, LAGS, step, 0)
    kept = factor_ref.shape[0]
    me = lax.axis_index("tm") * lax.axis_size("chan") + lax.axis_index("chan")
    first_row = pl.multiple_of(me * (columns // (lax.axis_size("tm") * lax.axis_size("chan"))) // kept * kept, kept)
    rows = work_ref[pl.ds(first_row, kept), :columns]
    row_id = lax.broadcasted_iota(jnp.int32, rows.shape, 0) + first_row
    col_id = lax.broadcasted_iota(jnp.int32, rows.shape, 1)
    factor_ref[...] = jnp.where(col_id >= row_id, rows, 0.0)


def whiten(sums, hankel, rows_all, kept):
    columns, count = hankel.shape
    return pl.pallas_call(
        functools.partial(whiten_kernel, rows_all),
        out_shape=(
            jax.ShapeDtypeStruct((kept, columns), jnp.float32),
            jax.ShapeDtypeStruct((columns, count), jnp.bfloat16),
        ),
        in_specs=[VMEM, VMEM],
        out_specs=(VMEM, VMEM),
        scratch_shapes=[
            pltpu.VMEM((columns, columns + count), jnp.float32),
            pltpu.VMEM((6 * columns // LAGS, columns), jnp.bfloat16),
            pltpu.VMEM((6 * columns // LAGS, columns + count), jnp.bfloat16),
        ],
        compiler_params=pltpu.CompilerParams(vmem_limit_bytes=48 * 2**20),
    )(sums, hankel)


def local(strain, fir_taps):
    samples = strain.shape[1]
    out_rows = samples // STRIDE
    rim = shifted(strain[:, :LANES], "tm", -1)
    decimated = decimate(strain, rim, fir_taps)
    gathered = lax.all_gather(decimated, "chan", axis=0, tiled=True)
    row_count = out_rows // lax.axis_size("chan")
    hankel, sums = hankel_and_sums(gathered, row_count)
    sums = summed(sums)
    devices_all = lax.axis_size(("tm", "chan"))
    columns = hankel.shape[0]
    factor_rows = columns // devices_all
    kept = max(8, factor_rows)
    factor, whitened = whiten(sums, hankel, row_count * devices_all, kept)
    if kept > factor_rows:
        first_row = lax.axis_index(("tm", "chan")) * factor_rows % kept
        factor = lax.dynamic_slice_in_dim(factor, first_row, factor_rows, 0)
    return (factor, whitened)


def solution(mesh):
    placed = (P("chan", "tm"), P("chan", None))
    return jax.shard_map(
        local,
        mesh=mesh,
        in_specs=placed,
        out_specs=(P(("tm", "chan"), None), P(None, ("tm", "chan"))),
        check_vma=False,
    )
```

```python
import functools

import jax
import jax.numpy as jnp
from jax import lax
from jax.experimental import pallas as pl
from jax.experimental.pallas import tpu as pltpu
from jax.sharding import PartitionSpec as P

LAGS = 8
TAPS = 64
STRIDE = 8
LANES = 128
MESH = pl.DeviceIdType.MESH
HIGHEST = lax.Precision.HIGHEST
VMEM = pl.BlockSpec(memory_space=pltpu.VMEM)


def shifted(value, axis, steps):
    count = lax.axis_size(axis)
    initial, last = (max(0, -steps), min(count, count - steps))
    return lax.ppermute(value, axis, [(source, source + steps) for source in range(initial, last)])


def decimate_kernel(strain_ref, rim_ref, taps_ref, out_ref, phase_ref):
    channels, samples = strain_ref.shape
    out_rows = samples // STRIDE
    width = STRIDE * LANES
    sample = lax.broadcasted_iota(jnp.int32, (width, width), 0)
    column = lax.broadcasted_iota(jnp.int32, (width, width), 1)
    wanted = STRIDE * (column % LANES) + column // LANES
    select = jnp.where(sample == wanted, 1.0, 0.0).astype(jnp.bfloat16)
    for g in range(out_rows // LANES + 1):
        if g < out_rows // LANES:
            part = jnp.dot(strain_ref[:, g * width : (g + 1) * width], select, preferred_element_type=jnp.float32)
        else:
            part = jnp.dot(rim_ref[...], select[:LANES], preferred_element_type=jnp.float32)
        for s in range(STRIDE):
            phase_ref[s, :, g * LANES : (g + 1) * LANES] = part[:, s * LANES : (s + 1) * LANES]
    span = out_rows + LANES
    for c in range(0, channels, 16):
        rows = slice(c, c + 16)
        total = jnp.zeros((16, span), jnp.float32)
        for j in range(TAPS // STRIDE):
            term = jnp.zeros((16, span), jnp.float32)
            for s in range(STRIDE):
                k = j * STRIDE + s
                term += taps_ref[rows, k : k + 1] * phase_ref[s, rows, :]
            total += term if j == 0 else pltpu.roll(term, span - j, 1)
        out_ref[rows, :] = total.astype(jnp.bfloat16)


def decimate(strain, rim, taps):
    channels, samples = strain.shape
    span = samples // STRIDE + LANES
    return pl.pallas_call(
        decimate_kernel,
        out_shape=jax.ShapeDtypeStruct((channels, span), jnp.bfloat16),
        in_specs=[VMEM] * 3,
        out_specs=VMEM,
        scratch_shapes=[pltpu.VMEM((STRIDE, channels, span), jnp.float32)],
        compiler_params=pltpu.CompilerParams(vmem_limit_bytes=40 * 2**20),
    )(strain, rim, taps)


def hankel_kernel(rows_ref, hankel_ref, sums_ref):
    group, first = lax.axis_index("tm"), lax.axis_index("chan")
    channels = rows_ref.shape[0]
    count = hankel_ref.shape[1]
    start = pl.multiple_of(first * count, LANES)
    window = rows_ref[:, pl.ds(start, count + LANES)].astype(jnp.float32)
    span = count + LANES
    for i in range(LAGS):
        moved = window if i == 0 else pltpu.roll(window, span - i, 1)
        hankel_ref[i * channels : (i + 1) * channels, :] = moved[:, :count].astype(jnp.bfloat16)
    leads = jnp.logical_and(group == 0, first == 0)
    skip = jnp.where(leads, LAGS - 1, 0)
    keep = lax.broadcasted_iota(jnp.int32, (channels, count), 1) >= skip
    left = jnp.where(keep, window[:, :count], 0.0).astype(jnp.bfloat16)
    sums_ref[:, : LAGS * channels] = lax.dot_general(
        left, hankel_ref[...], (((1,), (1,)), ((), ())), preferred_element_type=jnp.float32
    )
    lane = lax.broadcasted_iota(jnp.int32, (channels, LANES), 1)
    seen = jnp.where(leads, 2 * LAGS, 0)
    sums_ref[:, LAGS * channels :] = jnp.where(lane < seen, window[:, :LANES], 0.0)


def hankel_and_sums(rows, count):
    channels = rows.shape[0]
    return pl.pallas_call(
        hankel_kernel,
        out_shape=(
            jax.ShapeDtypeStruct((LAGS * channels, count), jnp.bfloat16),
            jax.ShapeDtypeStruct((channels, LAGS * channels + LANES), jnp.float32),
        ),
        in_specs=[VMEM],
        out_specs=(VMEM, VMEM),
        compiler_params=pltpu.CompilerParams(vmem_limit_bytes=40 * 2**20),
    )(rows)


def sum_kernel(near, mine_ref, out_ref, total, from_core, from_near, from_far, full, core_sem, near_sem, far_sem, all_sem, hand_sem):
    tm, chan = lax.axis_index("tm"), lax.axis_index("chan")
    far = lax.axis_size("tm") // near
    spot, place = lax.rem(tm, near), lax.div(tm, near)
    rows = mine_ref.shape[0]
    half = rows // 2
    piece = half // near
    core = {"chan": 1 - chan}

    def near_of(d):
        return lax.rem(spot + d, near)

    def near_id(d):
        return {"tm": place * near + near_of(d)}

    def far_id(d):
        return {"tm": lax.rem(place + d, far) * near + spot}

    def copy(source, target, sems, slot, device):
        return pltpu.make_async_remote_copy(
            src_ref=source,
            dst_ref=target,
            send_sem=sems.at[0, slot],
            recv_sem=sems.at[1, slot],
            device_id=device,
            device_id_type=MESH,
        )

    barrier = pltpu.get_barrier_semaphore()
    partners = [core] + [near_id(d) for d in range(1, near)] + [far_id(d) for d in range(1, far)]
    for partner in partners:
        pl.semaphore_signal(barrier, inc=1, device_id=partner, device_id_type=MESH)
    pl.semaphore_wait(barrier, len(partners))

    away = pl.ds(pl.multiple_of((1 - chan) * half, half), half)
    home = pl.ds(pl.multiple_of(chan * half, half), half)
    step = copy(mine_ref.at[away], from_core, core_sem, 0, core)
    step.start()
    step.wait()
    total[...] = mine_ref[home] + from_core[...]

    steps = []
    for d in range(1, near):
        part = total.at[pl.ds(pl.multiple_of(near_of(d) * piece, piece), piece)]
        steps.append(copy(part, from_near.at[d - 1], near_sem, d - 1, near_id(d)))
        steps[-1].start()
    own = total[pl.ds(pl.multiple_of(spot * piece, piece), piece)]
    for d in range(1, near):
        steps[d - 1].wait()
        own += from_near[d - 1]

    from_far[place] = own
    steps = []
    for d in range(1, far):
        steps.append(copy(from_far.at[place], from_far.at[place], far_sem, d - 1, far_id(d)))
        steps[-1].start()
    for step in steps:
        step.wait()
    own = from_far[0]
    for d in range(1, far):
        own += from_far[d]

    def at(spot_of):
        return pl.ds(pl.multiple_of(chan * half + spot_of * piece, piece), piece)

    full[at(spot)] = own
    steps = []
    for d in range(1, near):
        steps.append(copy(full.at[at(spot)], full.at[at(spot)], all_sem, d - 1, near_id(d)))
        steps[-1].start()
    hands = [copy(full.at[at(spot)], full.at[at(spot)], hand_sem, 0, core)]
    hands[0].start()
    for d in range(1, near):
        steps[d - 1].wait()
        came = at(lax.rem(spot - d + near, near))
        hands.append(copy(full.at[came], full.at[came], hand_sem, d, core))
        hands[-1].start()
    for hand in hands:
        hand.wait()
    out_ref[...] = full[...]


def summed(value):
    rows, columns = value.shape
    tm = lax.axis_size("tm")
    near = 4 if tm % 4 == 0 else 2
    far = tm // near
    half, piece = rows // 2, rows // 2 // near
    dtype = jnp.float32
    return pl.pallas_call(
        functools.partial(sum_kernel, near),
        out_shape=jax.ShapeDtypeStruct((rows, columns), dtype),
        in_specs=[VMEM],
        out_specs=VMEM,
        scratch_shapes=[
            pltpu.VMEM((half, columns), dtype),
            pltpu.VMEM((half, columns), dtype),
            pltpu.VMEM((near - 1, piece, columns), dtype),
            pltpu.VMEM((far, piece, columns), dtype),
            pltpu.VMEM((rows, columns), dtype),
            pltpu.SemaphoreType.DMA((2, 1)),
            pltpu.SemaphoreType.DMA((2, near - 1)),
            pltpu.SemaphoreType.DMA((2, max(far - 1, 1))),
            pltpu.SemaphoreType.DMA((2, near - 1)),
            pltpu.SemaphoreType.DMA((2, near)),
        ],
        compiler_params=pltpu.CompilerParams(
            collective_id=0, has_side_effects=True, vmem_limit_bytes=24 * 2**20
        ),
    )(value)


def factor_block(block):
    size = block.shape[0]
    row_id = lax.broadcasted_iota(jnp.int32, (size, size), 0)
    col_id = lax.broadcasted_iota(jnp.int32, (size, size), 1)
    sub = lax.broadcasted_iota(jnp.int32, (8, size), 0)
    low = block
    inv = jnp.where(row_id == col_id, 1.0, 0.0)
    factors, inverses = [], []
    for b in range(size // 8):
        cols = [jnp.broadcast_to(low[:, 8 * b + j : 8 * b + j + 1], low.shape) for j in range(8)]
        top, low = low[:8], low[8:]
        x_top, inv = inv[:8], inv[8:]
        c_top, c_low = [c[:8] for c in cols], [c[8:] for c in cols]
        scale = jnp.zeros((8, size), jnp.float32)
        more = b < size // 8 - 1
        for i in range(8):
            root = lax.rsqrt(jnp.broadcast_to(c_top[i][i : i + 1], (8, size)))
            over = root[:1] * root[:1]
            scale = jnp.where(sub == i, root, scale)
            below = jnp.where(sub > i, c_top[i], 0.0)
            row, x_row = top[i : i + 1] * over, x_top[i : i + 1] * over
            c_row = [c_top[j][i : i + 1] * over for j in range(i + 1, 8)]
            top, x_top = top - below * row, x_top - below * x_row
            for j in range(i + 1, 8):
                c_top[j] = c_top[j] - below * c_row[j - i - 1]
            if more:
                low, inv = low - c_low[i] * row, inv - c_low[i] * x_row
                for j in range(i + 1, 8):
                    c_low[j] = c_low[j] - c_low[i] * c_row[j - i - 1]
        factors.append(top * scale)
        inverses.append(x_top * scale)
    factor = jnp.concatenate(factors, axis=0)
    return jnp.where(col_id >= row_id, factor, 0.0), jnp.concatenate(inverses, axis=0)


def whiten_kernel(rows_all, sums_ref, hankel_ref, factor_ref, white_ref, work_ref, left_ref, right_ref):
    columns, count = hankel_ref.shape
    channels = columns // LAGS
    size = channels
    head = sums_ref[:, columns:]
    lane = lax.broadcasted_iota(jnp.int32, (channels, LANES), 1)
    heads = [(head if i == 0 else pltpu.roll(head, LANES - i, 1)).astype(jnp.bfloat16) for i in range(LAGS)]
    head_hankel = jnp.concatenate(heads, axis=0)
    scale = 1.0 / rows_all
    for i in range(LAGS):
        wide = columns - i * channels
        own = jnp.logical_and(lane >= i, lane < LAGS - 1)
        left = jnp.where(own, head, 0.0).astype(jnp.bfloat16)
        extra = lax.dot_general(
            left, head_hankel[:wide], (((1,), (1,)), ((), ())), preferred_element_type=jnp.float32
        )
        work_ref[i * channels : (i + 1) * channels, i * channels : columns] = (sums_ref[:, :wide] + extra) * scale
        if i:
            work_ref[i * channels : (i + 1) * channels, : i * channels] = jnp.zeros((channels, i * channels), jnp.float32)
    work_ref[:, columns:] = hankel_ref[...].astype(jnp.float32)

    def step(k, _):
        first = pl.multiple_of(k * size, size)
        mine = pl.ds(first, size)
        factor, inverse = factor_block(work_ref[mine, mine])
        solved = jnp.dot(inverse, work_ref[mine, :], preferred_element_type=jnp.float32, precision=HIGHEST)
        work_ref[mine, :] = solved
        work_ref[mine, mine] = factor
        white_ref[mine, :] = solved[:, columns:].astype(jnp.bfloat16)

        high = solved.astype(jnp.bfloat16)
        rest = solved - high.astype(jnp.float32)
        middle = rest.astype(jnp.bfloat16)
        little = (rest - middle.astype(jnp.float32)).astype(jnp.bfloat16)
        for n, (left, right) in enumerate(
            ((high, high), (high, middle), (middle, high), (middle, middle), (high, little), (little, high))
        ):
            left_ref[n * size : (n + 1) * size, :] = left[:, :columns]
            right_ref[n * size : (n + 1) * size, :] = right

        def update(start, i, _):
            other = pl.ds(pl.multiple_of(i * size, size), size)
            work_ref[other, start:] -= lax.dot_general(
                left_ref[:, other],
                right_ref[:, start:],
                (((0,), (0,)), ((), ())),
                preferred_element_type=jnp.float32,
            )
            return 0

        for q in range(0, LAGS, 2):
            initial, last = jnp.maximum(k + 1, q), jnp.maximum(k + 1, q + 2)
            lax.fori_loop(initial, last, functools.partial(update, q * size), 0)
        return 0

    lax.fori_loop(0, LAGS, step, 0)
    kept = factor_ref.shape[0]
    me = lax.axis_index("tm") * lax.axis_size("chan") + lax.axis_index("chan")
    first_row = pl.multiple_of(me * (columns // (lax.axis_size("tm") * lax.axis_size("chan"))) // kept * kept, kept)
    rows = work_ref[pl.ds(first_row, kept), :columns]
    row_id = lax.broadcasted_iota(jnp.int32, rows.shape, 0) + first_row
    col_id = lax.broadcasted_iota(jnp.int32, rows.shape, 1)
    factor_ref[...] = jnp.where(col_id >= row_id, rows, 0.0)


def whiten(sums, hankel, rows_all, kept):
    columns, count = hankel.shape
    return pl.pallas_call(
        functools.partial(whiten_kernel, rows_all),
        out_shape=(
            jax.ShapeDtypeStruct((kept, columns), jnp.float32),
            jax.ShapeDtypeStruct((columns, count), jnp.bfloat16),
        ),
        in_specs=[VMEM, VMEM],
        out_specs=(VMEM, VMEM),
        scratch_shapes=[
            pltpu.VMEM((columns, columns + count), jnp.float32),
            pltpu.VMEM((6 * columns // LAGS, columns), jnp.bfloat16),
            pltpu.VMEM((6 * columns // LAGS, columns + count), jnp.bfloat16),
        ],
        compiler_params=pltpu.CompilerParams(vmem_limit_bytes=48 * 2**20),
    )(sums, hankel)


def local(strain, fir_taps):
    samples = strain.shape[1]
    out_rows = samples // STRIDE
    rim = shifted(strain[:, :LANES], "tm", -1)
    decimated = decimate(strain, rim, fir_taps)
    gathered = lax.all_gather(decimated, "chan", axis=0, tiled=True)
    row_count = out_rows // lax.axis_size("chan")
    hankel, sums = hankel_and_sums(gathered, row_count)
    sums = summed(sums)
    devices_all = lax.axis_size(("tm", "chan"))
    columns = hankel.shape[0]
    factor_rows = columns // devices_all
    kept = max(8, factor_rows)
    factor, whitened = whiten(sums, hankel, row_count * devices_all, kept)
    if kept > factor_rows:
        first_row = lax.axis_index(("tm", "chan")) * factor_rows % kept
        factor = lax.dynamic_slice_in_dim(factor, first_row, factor_rows, 0)
    return (factor, whitened)


def solution(mesh):
    placed = (P("chan", "tm"), P("chan", None))
    return jax.shard_map(
        local,
        mesh=mesh,
        in_specs=placed,
        out_specs=(P(("tm", "chan"), None), P(None, ("tm", "chan"))),
        check_vma=False,
    )
```
